32 devices in a mesh: groups: 2 (over y), ctx: 16 (over z, x, core).
Axes of the slice: x: 2, y: 2, z: 4, core: 2. Of those that a mesh axis runs over, the one named last changes fastest.
Arguments:
- queries: bfloat16 [3072, 2048], P(('groups', 'ctx')), parts along dimension 0
- new_keys: bfloat16 [3072, 512], P(('groups', 'ctx')), parts along dimension 0
- new_values: bfloat16 [3072, 512], P(('groups', 'ctx')), parts along dimension 0, may hold values from -6 to 6
- prefix_keys: bfloat16 [512, 512], P(('groups', 'ctx')), parts along dimension 0, may hold values from -6 to 6
- prefix_values: bfloat16 [512, 512], P(('groups', 'ctx')), parts along dimension 0, may hold values from -6 to 6
- prefix_len: int32 [32], P(('groups', 'ctx')), parts along dimension 0, may hold values from 8 to 16, as said below
- owners: int32 [192], P(('groups', 'ctx')), parts along dimension 0, may hold values from 0 to 15, as said below
Outputs:
- attended: bfloat16 [3072, 2048], P(('groups', 'ctx')), parts along dimension 0
- log_mass: float32 [32, 1536], P('groups', 'ctx'), parts along dimension 0
- owned_cache: bfloat16 [384, 16, 1024], P(('groups', 'ctx')), parts along dimension 0
The draws below stay inside these ranges and needn't reach their ends.
There are 2 independent parts, one for each index of `groups`. The reference program is written for one: setup_inputs(seed, part) draws one part's arguments, and reference() takes and returns one part's arrays. A program takes and returns all parts, laid end to end along the dimension named above; each array names one. Nothing has to cross between parts.
Inputs may be any that keep to these rules, and one draw needn't show every extreme that they name: `prefix_len`: slots of a shard from its count on are stale; some shard has all 16 slots live. `owners`: each device owns at most 12 fresh blocks, and some device owns exactly 12.
All inputs are finite; a program needn't handle non-finite values.
Results may differ from the reference program's by a relative error of at most 0.0049.
Values may be sent and summed in bfloat16 or wider, within the bound.
A program may use at most 128 MiB of HBM per device.

```python
import math
import jax
import jax.numpy as jnp
from jax import lax

H = 16
G = 4
DH = 128
P_DEV = 16
BLK = 16
CAP = 12
NEW = 1536
PREFIX = 256
NBLK = 96
N_CTX = 16


def draw_queries(key, part):
    key = jax.random.fold_in(key, 1)
    values = 1.5 * jax.random.normal(key, (NEW, H * DH), jnp.float32)
    return values.astype(jnp.bfloat16)


def draw_new_keys(key, part):
    key = jax.random.fold_in(key, 2)
    values = jax.random.normal(key, (NEW, G * DH), jnp.float32)
    return values.astype(jnp.bfloat16)


def draw_prefix_len(key, part):
    key = jax.random.fold_in(key, 3)
    first, second = jax.random.split(key, 2)
    counts = jax.random.randint(first, (N_CTX,), P_DEV // 2, P_DEV + 1)
    full_shard = jax.random.randint(second, (), 0, N_CTX)
    counts = jnp.where(jnp.arange(N_CTX) == full_shard, P_DEV, counts)
    return counts.astype(jnp.int32)


def draw_owners(key, part):
    key = jax.random.fold_in(key, 4)
    first, second, third = jax.random.split(key, 3)
    slots_all = N_CTX * CAP
    shuffled = jax.random.permutation(first, slots_all)
    full_owner = jax.random.randint(second, (), 0, N_CTX)
    score = jnp.where(shuffled // CAP == full_owner, 0, 1) * slots_all + jnp.arange(slots_all)
    order = jnp.argsort(score, stable=True)
    chosen = shuffled[order][:NBLK]
    mixed = jax.random.permutation(third, chosen)
    return (mixed // CAP).astype(jnp.int32)


def block_scale(stream_key, shape, pieces, least, largest):
    factor_of, own = 1.0, jax.random.fold_in(stream_key, 6)
    for axis_at, blocks in pieces:
        draws = jnp.exp(jax.random.uniform(jax.random.fold_in(own, axis_at), (blocks,), jnp.float32, least / len(pieces), largest / len(pieces)))
        factor_of = factor_of * jnp.repeat(draws, shape[axis_at] // blocks).reshape([-1 if axis == axis_at else 1 for axis in range(len(shape))])
    return factor_of


def normal_values(own_key, shape, spread, most, cuts=(), kind=jnp.bfloat16):
    level = block_scale(own_key, shape, cuts, -0.22, 0.18) if cuts else 1.0
    values = jax.random.normal(own_key, shape, jnp.float32) * spread * level
    return jnp.minimum(jnp.maximum(values, -most), most).astype(kind)


def setup_inputs(seed: int = 0, part: int = 0) -> dict:
    splits = jax.random.split(jax.random.key(seed), 8)
    part_splits = jax.random.split(jax.random.fold_in(splits[7], part), 8)
    queries = draw_queries(jax.random.fold_in(jax.random.fold_in(splits[7], part), 71), part)
    new_keys = draw_new_keys(jax.random.fold_in(jax.random.fold_in(splits[7], part), 71), part)
    new_values = normal_values(part_splits[2], (NEW, G * DH), 1.0, 6.0, ((0, 16),))
    prefix_keys = normal_values(part_splits[3], (PREFIX, G * DH), 1.0, 6.0, ((0, 16),))
    prefix_values = normal_values(part_splits[4], (PREFIX, G * DH), 1.0, 6.0, ((0, 16),))
    prefix_len = draw_prefix_len(jax.random.fold_in(jax.random.fold_in(splits[7], part), 71), part)
    owners = draw_owners(jax.random.fold_in(jax.random.fold_in(splits[7], part), 71), part)
    return {"queries": queries, "new_keys": new_keys, "new_values": new_values, "prefix_keys": prefix_keys, "prefix_values": prefix_values, "prefix_len": prefix_len, "owners": owners}


def block_ranks(owner_list):
    count = owner_list.shape[0]
    same = owner_list[:, None] == owner_list[None, :]
    lower = jnp.arange(count)[None, :] < jnp.arange(count)[:, None]
    return jnp.sum((same & lower).astype(jnp.int32), axis=1).astype(jnp.int32)


def reference(queries, new_keys, new_values, prefix_keys, prefix_values, prefix_len, owners):
    per_group = H // G
    pre_rows = prefix_keys.shape[0]
    new_rows = new_keys.shape[0]
    all_keys = jnp.concatenate([prefix_keys, new_keys], 0).reshape(-1, G, DH).astype(jnp.float32)
    all_values = jnp.concatenate([prefix_values, new_values], 0).reshape(-1, G, DH).astype(jnp.float32)
    key_index = jnp.arange(pre_rows + new_rows).astype(jnp.int32)
    is_prefix = key_index < pre_rows
    key_token = key_index - pre_rows
    slot_live = (jnp.arange(pre_rows).astype(jnp.int32) % P_DEV) < jnp.repeat(prefix_len, P_DEV)
    live_all = jnp.concatenate([slot_live, jnp.zeros((new_rows,), bool)], 0)
    rows_step = math.gcd(new_rows, 256)

    def one_block(block_id):
        start = (block_id * rows_step).astype(jnp.int32)
        query_block = lax.dynamic_slice_in_dim(queries, start, rows_step, 0)
        query_block = query_block.reshape(rows_step, G, per_group, DH).astype(jnp.float32)
        query_token = start + jnp.arange(rows_step).astype(jnp.int32)
        visible = jnp.where(is_prefix[None, :], live_all[None, :],
                            key_token[None, :] <= query_token[:, None])
        scores = jnp.einsum('qgjd,kgd->gjqk', query_block, all_keys) * (DH ** -0.5)
        scores = jnp.where(visible[None, None], scores, -1e30)
        top = jnp.max(scores, axis=-1, keepdims=True)
        weights = jnp.where(visible[None, None], jnp.exp(scores - top), 0.0)
        total = jnp.sum(weights, axis=-1)
        rounded = lax.optimization_barrier(weights.astype(jnp.bfloat16))
        mixed = jnp.einsum('gjqk,kgd->gjqd', rounded.astype(jnp.float32), all_values)
        result = (mixed / total[..., None]).transpose(2, 0, 1, 3).reshape(rows_step, H * DH)
        log_total = (top[..., 0] + jnp.log(total)).reshape(H, rows_step)
        return result.astype(jnp.bfloat16), log_total.astype(jnp.float32)

    results, logs = lax.map(one_block, jnp.arange(new_rows // rows_step).astype(jnp.int32))
    attended = results.reshape(new_rows, H * DH)
    log_mass = logs.transpose(1, 0, 2).reshape(H, new_rows)

    block_count = owners.shape[0]
    ranks = block_ranks(owners)
    slot_of = owners * CAP + ranks
    slots_all = N_CTX * CAP
    match = slot_of[None, :] == jnp.arange(slots_all).astype(jnp.int32)[:, None]
    present = jnp.any(match, axis=1)
    wanted = jnp.sum(jnp.where(match, jnp.arange(block_count).astype(jnp.int32)[None, :], 0), axis=1).astype(jnp.int32)
    fresh_blocks = jnp.concatenate([new_keys, new_values], 1).reshape(block_count, BLK, 2 * G * DH)
    owned_cache = jnp.where(present[:, None, None], fresh_blocks[wanted], jnp.zeros((), jnp.bfloat16)).astype(jnp.bfloat16)
    return attended, log_mass, owned_cache
```

```python
import functools
import math

import jax
import jax.numpy as jnp
from jax import lax
from jax.experimental import pallas as pl
from jax.experimental.pallas import tpu as pltpu
from jax.sharding import PartitionSpec as P

MESH = pl.DeviceIdType.MESH

H = 16
G = 4
DH = 128
Q_DEV = 96
P_DEV = 16
BLK = 16
CAP = 12


def block_size(total_rows):
    return max((size for size in range(1, 1537) if total_rows % size == 0))


def per_device(queries, new_keys, new_values, prefix_keys, prefix_values, prefix_len, owners):
    per_group = H // G
    device_rank = lax.axis_index("ctx")
    cycle_size = lax.axis_size("ctx")
    all_owners, all_live = (
        lax.all_gather(owners, "ctx", axis=0, tiled=True),
        lax.all_gather(prefix_len, "ctx", axis=0, tiled=True),
    )
    block_count = all_owners.shape[0]
    same_owner = all_owners[:, None] == all_owners[None, :]
    lower = jnp.arange(block_count)[None, :] < jnp.arange(block_count)[:, None]
    ranks = jnp.sum((same_owner & lower).astype(jnp.int32), axis=1)
    match = (all_owners[None, :] == device_rank) & (ranks[None, :] == jnp.arange(CAP)[:, None])
    present = jnp.any(match, axis=1)
    wanted = jnp.sum(jnp.where(match, jnp.arange(block_count)[None, :], 0), axis=1)
    want_token = (wanted[:, None] * BLK + jnp.arange(BLK)[None, :]).reshape(-1)
    row_present = jnp.repeat(present, BLK)
    query_heads = queries.reshape(Q_DEV, G, per_group, DH)
    my_tokens = device_rank * Q_DEV + jnp.arange(Q_DEV)
    scale = DH ** (-0.5)

    def attend_rows(state, piece, global_start, pre_width, fresh_width):
        count_rows = piece.shape[0]
        row_index = global_start + jnp.arange(count_rows)
        width = pre_width + fresh_width
        shard_id = row_index // width
        offset = row_index % width
        is_prefix = offset < pre_width
        live_here = jnp.take(all_live, jnp.clip(shard_id, 0, cycle_size - 1))
        token_pos = shard_id * Q_DEV + offset - pre_width
        visible = jnp.where(
            is_prefix[None, :],
            (offset < live_here)[None, :],
            token_pos[None, :] <= my_tokens[:, None],
        )
        running, totals, accum = state
        keys_part = piece[:, : G * DH].reshape(count_rows, G, DH)
        values_part = piece[:, G * DH :].reshape(count_rows, G, DH)
        scores = (
            jnp.einsum("qgjd,kgd->gjqk", query_heads, keys_part, preferred_element_type=jnp.float32)
            * scale
        )
        scores = jnp.where(visible[None, None], scores, -1e30)
        new_top = jnp.maximum(running, jnp.max(scores, axis=-1))
        weights = jnp.where(visible[None, None], jnp.exp(scores - new_top[..., None]), 0.0)
        factor = jnp.exp(running - new_top)
        totals = totals * factor + jnp.sum(weights, axis=-1)
        accum = accum * factor[..., None] + jnp.einsum(
            "gjqk,kgd->gjqd",
            weights.astype(jnp.bfloat16),
            values_part,
            preferred_element_type=jnp.float32,
        )
        return (new_top, totals, accum)

    def fold_piece(state, piece, start, pre_width, fresh_width):
        count_rows = piece.shape[0]
        step_rows = block_size(count_rows)
        steps_count = count_rows // step_rows
        if steps_count == 1:
            return attend_rows(state, piece, start, pre_width, fresh_width)
        pieces = piece.reshape(steps_count, step_rows, piece.shape[1])

        def advance(carried, inputs):
            block_rows, block_id = inputs
            return (
                attend_rows(
                    carried, block_rows, start + block_id * step_rows, pre_width, fresh_width
                ),
                None,
            )

        state, unused = lax.scan(advance, state, (pieces, jnp.arange(steps_count)))
        return state

    start_state = (
        jnp.full((G, per_group, Q_DEV), -1e30, jnp.float32),
        jnp.zeros((G, per_group, Q_DEV), jnp.float32),
        jnp.zeros((G, per_group, Q_DEV, DH), jnp.float32),
    )
    owned_start = jnp.zeros((CAP * BLK, 2 * G * DH), jnp.bfloat16)
    prefix_rows = jnp.concatenate([prefix_keys, prefix_values], 1)
    fresh_rows = jnp.concatenate([new_keys, new_values], 1)
    stacked = jnp.concatenate([prefix_rows, fresh_rows], 0)
    carried = (start_state, owned_start)
    piece = lax.all_gather(stacked, "ctx", axis=0, tiled=True)
    state = fold_piece(carried[0], piece, jnp.int32(0), P_DEV, Q_DEV)
    count_rows = piece.shape[0]
    width = P_DEV + Q_DEV
    target = want_token // Q_DEV * width + P_DEV + want_token % Q_DEV
    inside = (target >= 0) & (target < count_rows) & row_present
    taken = jnp.take(piece, jnp.clip(target, 0, count_rows - 1), axis=0)
    owned = jnp.where(inside[:, None], taken, carried[1])
    running, totals, accum = state
    attended = (
        (accum / totals[..., None])
        .transpose(2, 0, 1, 3)
        .reshape(Q_DEV, H * DH)
        .astype(jnp.bfloat16)
    )
    log_mass = (running + jnp.log(totals)).reshape(H, Q_DEV)
    owned_cache = owned.reshape(CAP, BLK, 2 * G * DH)
    return (attended, log_mass, owned_cache)


PRE, KEY, VAL = range(3)
NEG = -1e30


def fused_kernel(
    A, B, q_hbm, k_ref, v_ref, pk_ref, pv_ref, len_ref, own_ref, out_ref, log_ref, cache_ref,
    q_buf, p_buf, k_buf, v_buf, qt, diff, top, total, accum, row_of, q_sem, send, recv,
):
    n = A * B * 2
    tokens, width = k_ref.shape
    prefix = pk_ref.shape[0]
    per_group = H // G
    lanes = per_group * tokens
    rows = 2 * tokens
    scale = DH ** (-0.5) * math.log2(math.e)
    group, me = lax.axis_index("groups"), lax.axis_index("ctx")
    c = me % 2
    b = (me // 2) % B
    a = me // (2 * B)
    up, down = me + 2 * B, me - 2 * B
    side, twin = me + 2 * (1 - 2 * b), me + 1 - 2 * c
    bufs = (p_buf, k_buf, v_buf)

    def shard(a_, b_, c_):
        return (a_ * B + b_) * 2 + c_

    def move(piece, slot, dest, sem):
        return pltpu.make_async_remote_copy(
            src_ref=bufs[piece].at[slot], dst_ref=bufs[piece].at[slot], send_sem=send.at[sem, slot, piece],
            recv_sem=recv.at[slot, piece], device_id=(group, dest), device_id_type=MESH,
        )

    def arrived(piece, slot):
        move(piece, slot, twin, 0).wait_recv()

    q_copy = pltpu.make_async_copy(q_hbm, q_buf, q_sem)
    q_copy.start()

    barrier = pltpu.get_barrier_semaphore()
    for dest in (side, twin):
        pl.semaphore_signal(barrier, inc=1, device_id=(group, dest), device_id_type=MESH)

    @pl.when(a < A - 1)
    def _():
        pl.semaphore_signal(barrier, inc=1, device_id=(group, up), device_id_type=MESH)

    @pl.when(a > 0)
    def _():
        pl.semaphore_signal(barrier, inc=1, device_id=(group, down), device_id_type=MESH)

    slot_id = lax.broadcasted_iota(jnp.int32, (prefix, DH), 0)
    lane = lax.broadcasted_iota(jnp.int32, (prefix, DH), 1)
    owner_row = jnp.full((prefix, DH), -1, jnp.int32)
    for j in range(own_ref.shape[0]):
        owner_row = jnp.where(lane // BLK == j, own_ref[j], owner_row)
    p_buf[me, :, 0:width] = pk_ref[...]
    p_buf[me, :, width : 2 * width] = pv_ref[...]
    live = jnp.where(slot_id < len_ref[0], 1.0, 0.0)
    p_buf[me, :, 2 * width : 2 * width + DH] = live.astype(jnp.bfloat16)
    p_buf[me, :, 2 * width + DH :] = owner_row.astype(jnp.float32).astype(jnp.bfloat16)
    k_buf[me] = k_ref[...]
    v_buf[me] = v_ref[...]

    pl.semaphore_wait(barrier, 2 + jnp.where(a < A - 1, 1, 0) + jnp.where(a > 0, 1, 0))

    def from_below(piece, slot):
        @pl.when(a < A - 1)
        def _():
            move(piece, slot, up, 0).start()

        move(piece, slot, side, 2).start()
        move(piece, slot, twin, 3).start()

    def from_above(piece, slot):
        @pl.when(a > 0)
        def _():
            move(piece, slot, down, 1).start()

        move(piece, slot, side, 2).start()
        move(piece, slot, twin, 3).start()

    for piece in (PRE, KEY, VAL):
        from_below(piece, me)

        @pl.when(a > 0)
        def _():
            move(piece, me, down, 1).start()

    q_copy.wait()
    for g in range(G):
        heads = [q_buf[:, (g * per_group + j) * DH : (g * per_group + j + 1) * DH] for j in range(per_group)]
        qt[g] = jnp.concatenate(heads, 0).T
    diff[...] = lax.broadcasted_iota(jnp.int32, (rows, lanes), 0) - lax.broadcasted_iota(jnp.int32, (rows, lanes), 1) % tokens
    top[...] = jnp.full(top.shape, NEG, jnp.float32)
    total[...] = jnp.zeros(total.shape, jnp.float32)
    accum[...] = jnp.zeros(accum.shape, jnp.float32)

    def fold(g, keys, values, visible):
        s = jnp.dot(keys, qt[g], preferred_element_type=jnp.float32) * scale
        s = jnp.where(visible, s, NEG)
        old = top[g : g + 1]
        new = jnp.maximum(old, jnp.max(s, axis=0, keepdims=True))
        w = jnp.exp2(s - new)
        factor = jnp.exp2(old - new)
        top[g : g + 1] = new
        total[g : g + 1] = total[g : g + 1] * factor + jnp.sum(w, axis=0, keepdims=True)
        mixed = lax.dot_general(
            values, w.astype(jnp.bfloat16), (((0,), (0,)), ((), ())), preferred_element_type=jnp.float32
        )
        accum[g] = accum[g] * factor + mixed

    def attend(unit):
        limit = me * tokens - unit * rows
        for g in range(G):
            at = slice(g * DH, (g + 1) * DH)
            keys = k_buf[pl.ds(2 * unit, 2), :, at].reshape(rows, DH)
            values = v_buf[pl.ds(2 * unit, 2), :, at].reshape(rows, DH)
            fold(g, keys, values, diff[...] <= limit)

    def relay(piece, slot):
        arrived(piece, slot)
        move(piece, slot, twin, 3).start()

    relay(PRE, shard(a, 1 - b, c))

    def stage(e, carry):
        d = e + 1

        @pl.when(a >= e)
        def _():
            for piece in (KEY, VAL):
                arrived(piece, shard(a - e, b, 1 - c))
            attend((a - e) * B + b)

        for piece in (PRE, KEY, VAL):
            @pl.when(a >= d)
            def _():
                arrived(piece, shard(a - d, b, c))
                from_below(piece, shard(a - d, b, c))

            @pl.when(a + d < A)
            def _():
                arrived(piece, shard(a + d, b, c))
                from_above(piece, shard(a + d, b, c))

        @pl.when(a >= d)
        def _():
            relay(PRE, shard(a - d, 1 - b, c))

        @pl.when(a + d < A)
        def _():
            relay(PRE, shard(a + d, 1 - b, c))

        for piece in (KEY, VAL):
            @pl.when(a >= e)
            def _():
                relay(piece, shard(a - e, 1 - b, c))

            @pl.when((a + e < A) & (e > 0))
            def _():
                relay(piece, shard(a + e, 1 - b, c))

        @pl.when(a >= e)
        def _():
            for piece in (KEY, VAL):
                arrived(piece, shard(a - e, 1 - b, 1 - c))

        @pl.when((a >= e) & ((e > 0) | (b > 0)))
        def _():
            attend((a - e) * B + 1 - b)

        @pl.when(e == A - 2)
        def _():
            attend_prefix()

        return carry

    def attend_prefix():
        for a_ in range(A):
            for b_ in range(B):
                arrived(PRE, shard(a_, b_, 1 - c))
        count = n * prefix
        whole = lambda lo, hi: p_buf[:, :, lo:hi].reshape(count, hi - lo)
        alive = whole(2 * width, 2 * width + DH).astype(jnp.float32)
        alive = jnp.concatenate([alive] * (lanes // DH), 1) > 0.5
        for g in range(G):
            lo = g * DH
            fold(g, whole(lo, lo + DH), whole(width + lo, width + lo + DH), alive)
        owner = whole(2 * width + DH, 2 * width + 2 * DH).astype(jnp.float32)
        mine = owner == me.astype(jnp.float32)
        flag = jnp.where(mine, 1.0, 0.0).astype(jnp.bfloat16)
        share = 1.0 / BLK
        from_, to = (lax.broadcasted_iota(jnp.int32, (DH, DH), i) // BLK for i in range(2))
        before = jnp.where(from_ < to, share, 0.0).astype(jnp.bfloat16)
        at, other = (lax.broadcasted_iota(jnp.int32, (count, count), i) // prefix for i in range(2))
        earlier = jnp.where(other < at, 1.0 / prefix, 0.0).astype(jnp.bfloat16)
        inside = jnp.dot(flag, before, preferred_element_type=jnp.float32)
        past = jnp.dot(earlier, flag, preferred_element_type=jnp.float32).astype(jnp.bfloat16)
        past = jnp.dot(past, jnp.full((DH, DH), share, jnp.bfloat16), preferred_element_type=jnp.float32)
        lane_ = lax.broadcasted_iota(jnp.int32, (count, DH), 1)
        place = (inside + past) * BLK + (lane_ % BLK).astype(jnp.float32)
        place = jnp.where(mine, place, -1.0)
        row_of[...] = jnp.concatenate([place[j * prefix : j * prefix + 8, :tokens] for j in range(n)], 1)

    lax.fori_loop(0, A, stage, 0)

    for g in range(G):
        result = (accum[g] / total[g : g + 1]).T
        mass = top[g : g + 1] * math.log(2) + jnp.log(total[g : g + 1])
        for j in range(per_group):
            h = g * per_group + j
            out_ref[:, h * DH : (h + 1) * DH] = result[j * tokens : (j + 1) * tokens].astype(jnp.bfloat16)
            log_ref[h : h + 1] = mass[:, j * tokens : (j + 1) * tokens]

    for a_ in range(A):
        for b_ in range(B):
            @pl.when((a_ > a) )
            def _():
                for piece in (KEY, VAL):
                    arrived(piece, shard(a_, b_, 1 - c))

    slots = cache_ref.shape[0] * BLK
    hot = lax.broadcasted_iota(jnp.int32, (slots, n * tokens), 0).astype(jnp.float32) == row_of[0:1]
    hot = jnp.where(hot, 1.0, 0.0).astype(jnp.bfloat16)
    for at, buf in ((0, k_buf), (width, v_buf)):
        rows_ = buf[...].reshape(n * tokens, width)
        picked = jnp.dot(hot, rows_, preferred_element_type=jnp.float32).astype(jnp.bfloat16)
        cache_ref[:, :, at : at + width] = picked.reshape(slots // BLK, BLK, width)

    for piece in (PRE, KEY, VAL):
        for a_ in range(A):
            slot = shard(a_, b, c)

            @pl.when((a_ <= a) & (a < A - 1))
            def _():
                move(piece, slot, up, 0).wait_send()

            @pl.when((a_ >= a) & (a > 0))
            def _():
                move(piece, slot, down, 1).wait_send()

            move(piece, slot, side, 2).wait_send()
            move(piece, slot, twin, 3).wait_send()
            move(piece, shard(a_, 1 - b, c), twin, 3).wait_send()


def fused(A, B, queries, new_keys, new_values, prefix_keys, prefix_values, prefix_len, owners):
    n = A * B * 2
    tokens, width = new_keys.shape
    prefix = prefix_keys.shape[0]
    lanes = H // G * tokens
    bf16, f32 = jnp.bfloat16, jnp.float32
    vmem, smem = pl.BlockSpec(memory_space=pltpu.VMEM), pl.BlockSpec(memory_space=pltpu.SMEM)
    return pl.pallas_call(
        functools.partial(fused_kernel, A, B),
        out_shape=(
            jax.ShapeDtypeStruct((tokens, H * DH), bf16),
            jax.ShapeDtypeStruct((H, tokens), f32),
            jax.ShapeDtypeStruct((CAP, BLK, 2 * width), bf16),
        ),
        in_specs=[pl.BlockSpec(memory_space=pl.ANY), vmem, vmem, vmem, vmem, smem, smem],
        out_specs=(vmem, vmem, vmem),
        scratch_shapes=[
            pltpu.VMEM((tokens, H * DH), bf16),
            pltpu.VMEM((n, prefix, 2 * width + 2 * DH), bf16),
            pltpu.VMEM((n, tokens, width), bf16),
            pltpu.VMEM((n, tokens, width), bf16),
            pltpu.VMEM((G, DH, lanes), bf16),
            pltpu.VMEM((2 * tokens, lanes), jnp.int32),
            pltpu.VMEM((8, lanes), f32),
            pltpu.VMEM((8, lanes), f32),
            pltpu.VMEM((G, DH, lanes), f32),
            pltpu.VMEM((8, n * tokens), f32),
            pltpu.SemaphoreType.DMA,
            pltpu.SemaphoreType.DMA((4, n, 3)),
            pltpu.SemaphoreType.DMA((n, 3)),
        ],
        compiler_params=pltpu.CompilerParams(
            collective_id=0, has_side_effects=True, vmem_limit_bytes=40 * 1024 * 1024
        ),
    )(queries, new_keys, new_values, prefix_keys, prefix_values, prefix_len, owners)


def solution(mesh):
    A = 4
    B = mesh.shape["ctx"] // (2 * A)
    body = functools.partial(fused, A, B) if B == 2 else per_device
    return jax.shard_map(
        body,
        mesh=mesh,
        in_specs=(
            P(("groups", "ctx"), None),
            P(("groups", "ctx"), None),
            P(("groups", "ctx"), None),
            P(("groups", "ctx"), None),
            P(("groups", "ctx"), None),
            P(("groups", "ctx")),
            P(("groups", "ctx")),
        ),
        out_specs=(
            P(("groups", "ctx"), None),
            P("groups", "ctx"),
            P(("groups", "ctx"), None, None),
        ),
        check_vma=False,
    )
```

```python
import functools
import math

import jax
import jax.numpy as jnp
from jax import lax
from jax.experimental import pallas as pl
from jax.experimental.pallas import tpu as pltpu
from jax.sharding import PartitionSpec as P

MESH = pl.DeviceIdType.MESH

H = 16
G = 4
DH = 128
Q_DEV = 96
P_DEV = 16
BLK = 16
CAP = 12


def block_size(total_rows):
    return max((size for size in range(1, 1537) if total_rows % size == 0))


def per_device(queries, new_keys, new_values, prefix_keys, prefix_values, prefix_len, owners):
    per_group = H // G
    device_rank = lax.axis_index("ctx")
    cycle_size = lax.axis_size("ctx")
    all_owners, all_live = (
        lax.all_gather(owners, "ctx", axis=0, tiled=True),
        lax.all_gather(prefix_len, "ctx", axis=0, tiled=True),
    )
    block_count = all_owners.shape[0]
    same_owner = all_owners[:, None] == all_owners[None, :]
    lower = jnp.arange(block_count)[None, :] < jnp.arange(block_count)[:, None]
    ranks = jnp.sum((same_owner & lower).astype(jnp.int32), axis=1)
    match = (all_owners[None, :] == device_rank) & (ranks[None, :] == jnp.arange(CAP)[:, None])
    present = jnp.any(match, axis=1)
    wanted = jnp.sum(jnp.where(match, jnp.arange(block_count)[None, :], 0), axis=1)
    want_token = (wanted[:, None] * BLK + jnp.arange(BLK)[None, :]).reshape(-1)
    row_present = jnp.repeat(present, BLK)
    query_heads = queries.reshape(Q_DEV, G, per_group, DH)
    my_tokens = device_rank * Q_DEV + jnp.arange(Q_DEV)
    scale = DH ** (-0.5)

    def attend_rows(state, piece, global_start, pre_width, fresh_width):
        count_rows = piece.shape[0]
        row_index = global_start + jnp.arange(count_rows)
        width = pre_width + fresh_width
        shard_id = row_index // width
        offset = row_index % width
        is_prefix = offset < pre_width
        live_here = jnp.take(all_live, jnp.clip(shard_id, 0, cycle_size - 1))
        token_pos = shard_id * Q_DEV + offset - pre_width
        visible = jnp.where(
            is_prefix[None, :],
            (offset < live_here)[None, :],
            token_pos[None, :] <= my_tokens[:, None],
        )
        running, totals, accum = state
        keys_part = piece[:, : G * DH].reshape(count_rows, G, DH)
        values_part = piece[:, G * DH :].reshape(count_rows, G, DH)
        scores = (
            jnp.einsum("qgjd,kgd->gjqk", query_heads, keys_part, preferred_element_type=jnp.float32)
            * scale
        )
        scores = jnp.where(visible[None, None], scores, -1e30)
        new_top = jnp.maximum(running, jnp.max(scores, axis=-1))
        weights = jnp.where(visible[None, None], jnp.exp(scores - new_top[..., None]), 0.0)
        factor = jnp.exp(running - new_top)
        totals = totals * factor + jnp.sum(weights, axis=-1)
        accum = accum * factor[..., None] + jnp.einsum(
            "gjqk,kgd->gjqd",
            weights.astype(jnp.bfloat16),
            values_part,
            preferred_element_type=jnp.float32,
        )
        return (new_top, totals, accum)

    def fold_piece(state, piece, start, pre_width, fresh_width):
        count_rows = piece.shape[0]
        step_rows = block_size(count_rows)
        steps_count = count_rows // step_rows
        if steps_count == 1:
            return attend_rows(state, piece, start, pre_width, fresh_width)
        pieces = piece.reshape(steps_count, step_rows, piece.shape[1])

        def advance(carried, inputs):
            block_rows, block_id = inputs
            return (
                attend_rows(
                    carried, block_rows, start + block_id * step_rows, pre_width, fresh_width
                ),
                None,
            )

        state, unused = lax.scan(advance, state, (pieces, jnp.arange(steps_count)))
        return state

    start_state = (
        jnp.full((G, per_group, Q_DEV), -1e30, jnp.float32),
        jnp.zeros((G, per_group, Q_DEV), jnp.float32),
        jnp.zeros((G, per_group, Q_DEV, DH), jnp.float32),
    )
    owned_start = jnp.zeros((CAP * BLK, 2 * G * DH), jnp.bfloat16)
    prefix_rows = jnp.concatenate([prefix_keys, prefix_values], 1)
    fresh_rows = jnp.concatenate([new_keys, new_values], 1)
    stacked = jnp.concatenate([prefix_rows, fresh_rows], 0)
    carried = (start_state, owned_start)
    piece = lax.all_gather(stacked, "ctx", axis=0, tiled=True)
    state = fold_piece(carried[0], piece, jnp.int32(0), P_DEV, Q_DEV)
    count_rows = piece.shape[0]
    width = P_DEV + Q_DEV
    target = want_token // Q_DEV * width + P_DEV + want_token % Q_DEV
    inside = (target >= 0) & (target < count_rows) & row_present
    taken = jnp.take(piece, jnp.clip(target, 0, count_rows - 1), axis=0)
    owned = jnp.where(inside[:, None], taken, carried[1])
    running, totals, accum = state
    attended = (
        (accum / totals[..., None])
        .transpose(2, 0, 1, 3)
        .reshape(Q_DEV, H * DH)
        .astype(jnp.bfloat16)
    )
    log_mass = (running + jnp.log(totals)).reshape(H, Q_DEV)
    owned_cache = owned.reshape(CAP, BLK, 2 * G * DH)
    return (attended, log_mass, owned_cache)


PRE, KEY, VAL = range(3)
NEG = -1e30
VMEM_BYTES = 40 * 1024 * 1024


def fused_kernel(
    A, B, q_hbm, k_ref, v_ref, pk_ref, pv_ref, len_hbm, own_hbm, out_ref, log_ref, cache_ref,
    q_buf, p_buf, k_buf, v_buf, len_ref, own_ref, qt, diff, top, total, accum, row_of, load, send, recv,
):
    n = A * B * 2
    tokens, width = k_ref.shape
    prefix = pk_ref.shape[0]
    per_group = H // G
    lanes = per_group * tokens
    rows = 2 * tokens
    scale = DH ** (-0.5) * math.log2(math.e)
    group, me = lax.axis_index("groups"), lax.axis_index("ctx")
    c = me % 2
    b = (me // 2) % B
    a = me // (2 * B)
    up, down = me + 2 * B, me - 2 * B
    side, twin = me + 2 * (1 - 2 * b), me + 1 - 2 * c
    bufs = (p_buf, k_buf, v_buf)

    def shard(a_, b_, c_):
        return (a_ * B + b_) * 2 + c_

    def move(piece, slot, dest, sem):
        return pltpu.make_async_remote_copy(
            src_ref=bufs[piece].at[slot], dst_ref=bufs[piece].at[slot], send_sem=send.at[sem, slot, piece],
            recv_sem=recv.at[slot, piece], device_id=(group, dest), device_id_type=MESH,
        )

    def arrived(piece, slot):
        move(piece, slot, twin, 0).wait_recv()

    loads = [
        pltpu.make_async_copy(src, dst, load.at[i])
        for i, (src, dst) in enumerate((
            (own_hbm, own_ref), (len_hbm, len_ref),
            (k_ref, k_buf.at[me]), (v_ref, v_buf.at[me]),
            (pk_ref, p_buf.at[me, :, 0:width]), (pv_ref, p_buf.at[me, :, width : 2 * width]), (q_hbm, q_buf),
        ))
    ]
    for copy in loads:
        copy.start()

    barrier = pltpu.get_barrier_semaphore()
    for dest in (side, twin):
        pl.semaphore_signal(barrier, inc=1, device_id=(group, dest), device_id_type=MESH)

    @pl.when(a < A - 1)
    def _():
        pl.semaphore_signal(barrier, inc=1, device_id=(group, up), device_id_type=MESH)

    @pl.when(a > 0)
    def _():
        pl.semaphore_signal(barrier, inc=1, device_id=(group, down), device_id_type=MESH)

    slot_id = lax.broadcasted_iota(jnp.int32, (prefix, DH), 0)
    lane = lax.broadcasted_iota(jnp.int32, (prefix, DH), 1)
    loads[0].wait()
    loads[1].wait()
    owner_row = jnp.full((prefix, DH), -1, jnp.int32)
    for j in range(own_ref.shape[0]):
        owner_row = jnp.where(lane // BLK == j, own_ref[j], owner_row)
    live = jnp.where(slot_id < len_ref[0], 1.0, 0.0)
    p_buf[me, :, 2 * width : 2 * width + DH] = live.astype(jnp.bfloat16)
    p_buf[me, :, 2 * width + DH :] = owner_row.astype(jnp.float32).astype(jnp.bfloat16)

    pl.semaphore_wait(barrier, 2 + jnp.where(a < A - 1, 1, 0) + jnp.where(a > 0, 1, 0))

    def from_below(piece, slot):
        @pl.when(a < A - 1)
        def _():
            move(piece, slot, up, 0).start()

        move(piece, slot, side, 2).start()
        move(piece, slot, twin, 3).start()

    def from_above(piece, slot):
        @pl.when(a > 0)
        def _():
            move(piece, slot, down, 1).start()

        move(piece, slot, side, 2).start()
        move(piece, slot, twin, 3).start()

    for piece, needs in ((KEY, loads[2:3]), (PRE, loads[4:6]), (VAL, loads[3:4])):
        for copy in needs:
            copy.wait()
        from_below(piece, me)

        @pl.when(a > 0)
        def _():
            move(piece, me, down, 1).start()

    loads[6].wait()
    for g in range(G):
        heads = [q_buf[:, (g * per_group + j) * DH : (g * per_group + j + 1) * DH] for j in range(per_group)]
        qt[g] = jnp.concatenate(heads, 0).T
    diff[...] = lax.broadcasted_iota(jnp.int32, (rows, lanes), 0) - lax.broadcasted_iota(jnp.int32, (rows, lanes), 1) % tokens
    top[...] = jnp.full(top.shape, NEG, jnp.float32)
    total[...] = jnp.zeros(total.shape, jnp.float32)
    accum[...] = jnp.zeros(accum.shape, jnp.float32)

    def fold(g, keys, values, visible):
        s = jnp.dot(keys, qt[g], preferred_element_type=jnp.float32) * scale
        s = jnp.where(visible, s, NEG)
        old = top[g : g + 1]
        new = jnp.maximum(old, jnp.max(s, axis=0, keepdims=True))
        w = jnp.exp2(s - new)
        factor = jnp.exp2(old - new)
        top[g : g + 1] = new
        total[g : g + 1] = total[g : g + 1] * factor + jnp.sum(w, axis=0, keepdims=True)
        mixed = lax.dot_general(
            values, w.astype(jnp.bfloat16), (((0,), (0,)), ((), ())), preferred_element_type=jnp.float32
        )
        accum[g] = accum[g] * factor + mixed

    def attend(unit):
        limit = me * tokens - unit * rows
        for g in range(G):
            at = slice(g * DH, (g + 1) * DH)
            keys = k_buf[pl.ds(2 * unit, 2), :, at].reshape(rows, DH)
            values = v_buf[pl.ds(2 * unit, 2), :, at].reshape(rows, DH)
            fold(g, keys, values, diff[...] <= limit)

    def relay(piece, slot):
        arrived(piece, slot)
        move(piece, slot, twin, 3).start()

    relay(PRE, shard(a, 1 - b, c))

    def stage(e, carry):
        d = e + 1

        @pl.when(a >= e)
        def _():
            for piece in (KEY, VAL):
                arrived(piece, shard(a - e, b, 1 - c))
            attend((a - e) * B + b)

        for piece in (PRE, KEY, VAL):
            @pl.when(a >= d)
            def _():
                arrived(piece, shard(a - d, b, c))
                from_below(piece, shard(a - d, b, c))

            @pl.when(a + d < A)
            def _():
                arrived(piece, shard(a + d, b, c))
                from_above(piece, shard(a + d, b, c))

        @pl.when(a >= d)
        def _():
            relay(PRE, shard(a - d, 1 - b, c))

        @pl.when(a + d < A)
        def _():
            relay(PRE, shard(a + d, 1 - b, c))

        for piece in (KEY, VAL):
            @pl.when(a >= e)
            def _():
                relay(piece, shard(a - e, 1 - b, c))

            @pl.when((a + e < A) & (e > 0))
            def _():
                relay(piece, shard(a + e, 1 - b, c))

        @pl.when(a >= e)
        def _():
            for piece in (KEY, VAL):
                arrived(piece, shard(a - e, 1 - b, 1 - c))

        @pl.when((a >= e) & ((e > 0) | (b > 0)))
        def _():
            attend((a - e) * B + 1 - b)

        @pl.when(e == A - 2)
        def _():
            attend_prefix()

        return carry

    def attend_prefix():
        for a_ in range(A):
            for b_ in range(B):
                arrived(PRE, shard(a_, b_, 1 - c))
        count = n * prefix
        whole = lambda lo, hi: p_buf[:, :, lo:hi].reshape(count, hi - lo)
        alive = whole(2 * width, 2 * width + DH).astype(jnp.float32)
        alive = jnp.concatenate([alive] * (lanes // DH), 1) > 0.5
        for g in range(G):
            lo = g * DH
            fold(g, whole(lo, lo + DH), whole(width + lo, width + lo + DH), alive)
        owner = whole(2 * width + DH, 2 * width + 2 * DH).astype(jnp.float32)
        mine = owner == me.astype(jnp.float32)
        flag = jnp.where(mine, 1.0, 0.0).astype(jnp.bfloat16)
        share = 1.0 / BLK
        from_, to = (lax.broadcasted_iota(jnp.int32, (DH, DH), i) // BLK for i in range(2))
        before = jnp.where(from_ < to, share, 0.0).astype(jnp.bfloat16)
        at, other = (lax.broadcasted_iota(jnp.int32, (count, count), i) // prefix for i in range(2))
        earlier = jnp.where(other < at, 1.0 / prefix, 0.0).astype(jnp.bfloat16)
        inside = jnp.dot(flag, before, preferred_element_type=jnp.float32)
        past = jnp.dot(earlier, flag, preferred_element_type=jnp.float32).astype(jnp.bfloat16)
        past = jnp.dot(past, jnp.full((DH, DH), share, jnp.bfloat16), preferred_element_type=jnp.float32)
        lane_ = lax.broadcasted_iota(jnp.int32, (count, DH), 1)
        place = (inside + past) * BLK + (lane_ % BLK).astype(jnp.float32)
        place = jnp.where(mine, place, -1.0)
        row_of[...] = jnp.concatenate([place[j * prefix : j * prefix + 8, :tokens] for j in range(n)], 1)

    lax.fori_loop(0, A, stage, 0)

    for g in range(G):
        result = (accum[g] / total[g : g + 1]).T
        mass = top[g : g + 1] * math.log(2) + jnp.log(total[g : g + 1])
        for j in range(per_group):
            h = g * per_group + j
            out_ref[:, h * DH : (h + 1) * DH] = result[j * tokens : (j + 1) * tokens].astype(jnp.bfloat16)
            log_ref[h : h + 1] = mass[:, j * tokens : (j + 1) * tokens]

    for a_ in range(A):
        for b_ in range(B):
            @pl.when(a_ > a)
            def _():
                for piece in (KEY, VAL):
                    arrived(piece, shard(a_, b_, 1 - c))

    slots = cache_ref.shape[0] * BLK
    hot = lax.broadcasted_iota(jnp.int32, (slots, n * tokens), 0).astype(jnp.float32) == row_of[0:1]
    hot = jnp.where(hot, 1.0, 0.0).astype(jnp.bfloat16)
    for at, buf in ((0, k_buf), (width, v_buf)):
        rows_ = buf[...].reshape(n * tokens, width)
        picked = jnp.dot(hot, rows_, preferred_element_type=jnp.float32).astype(jnp.bfloat16)
        cache_ref[:, :, at : at + width] = picked.reshape(slots // BLK, BLK, width)

    for piece in (PRE, KEY, VAL):
        for a_ in range(A):
            slot = shard(a_, b, c)

            @pl.when((a_ <= a) & (a < A - 1))
            def _():
                move(piece, slot, up, 0).wait_send()

            @pl.when((a_ >= a) & (a > 0))
            def _():
                move(piece, slot, down, 1).wait_send()

            move(piece, slot, side, 2).wait_send()
            move(piece, slot, twin, 3).wait_send()
            move(piece, shard(a_, 1 - b, c), twin, 3).wait_send()


def write_results(*refs):
    copies = [pltpu.make_async_copy(refs[i], refs[3 + i], refs[6].at[i]) for i in range(3)]
    for copy in copies:
        copy.start()
    for copy in copies:
        copy.wait()


def fused(A, B, queries, new_keys, new_values, prefix_keys, prefix_values, prefix_len, owners):
    n = A * B * 2
    tokens, width = new_keys.shape
    prefix = prefix_keys.shape[0]
    lanes = H // G * tokens
    bf16, f32 = jnp.bfloat16, jnp.float32
    vmem, hbm = pl.BlockSpec(memory_space=pltpu.VMEM), pl.BlockSpec(memory_space=pltpu.HBM)
    arrays = (queries, new_keys, new_values, prefix_keys, prefix_values)
    results = pl.pallas_call(
        functools.partial(fused_kernel, A, B),
        out_shape=(
            jax.ShapeDtypeStruct((tokens, H * DH), bf16),
            jax.ShapeDtypeStruct((H, tokens), f32),
            jax.ShapeDtypeStruct((CAP, BLK, 2 * width), bf16),
        ),
        in_specs=[hbm] * 7,
        out_specs=(vmem,) * 3,
        scratch_shapes=[
            pltpu.VMEM((tokens, H * DH), bf16),
            pltpu.VMEM((n, prefix, 2 * width + 2 * DH), bf16),
            pltpu.VMEM((n, tokens, width), bf16),
            pltpu.VMEM((n, tokens, width), bf16),
            pltpu.SMEM(prefix_len.shape, jnp.int32),
            pltpu.SMEM(owners.shape, jnp.int32),
            pltpu.VMEM((G, DH, lanes), bf16),
            pltpu.VMEM((2 * tokens, lanes), jnp.int32),
            pltpu.VMEM((8, lanes), f32),
            pltpu.VMEM((8, lanes), f32),
            pltpu.VMEM((G, DH, lanes), f32),
            pltpu.VMEM((8, n * tokens), f32),
            pltpu.SemaphoreType.DMA((7,)),
            pltpu.SemaphoreType.DMA((4, n, 3)),
            pltpu.SemaphoreType.DMA((n, 3)),
        ],
        compiler_params=pltpu.CompilerParams(
            collective_id=0, has_side_effects=True, vmem_limit_bytes=VMEM_BYTES
        ),
    )(*(pltpu.with_memory_space_constraint(x, pltpu.HBM) for x in arrays), prefix_len, pltpu.with_memory_space_constraint(owners, pltpu.HBM))
    return pl.pallas_call(
        write_results,
        out_shape=tuple(jax.ShapeDtypeStruct(x.shape, x.dtype) for x in results),
        in_specs=[vmem] * 3,
        out_specs=(hbm,) * 3,
        scratch_shapes=[pltpu.SemaphoreType.DMA((3,))],
    )(*results)


def solution(mesh):
    A = 4
    B = mesh.shape["ctx"] // (2 * A)
    body = functools.partial(fused, A, B) if B == 2 else per_device
    return jax.shard_map(
        body,
        mesh=mesh,
        in_specs=(
            P(("groups", "ctx"), None),
            P(("groups", "ctx"), None),
            P(("groups", "ctx"), None),
            P(("groups", "ctx"), None),
            P(("groups", "ctx"), None),
            P(("groups", "ctx")),
            P(("groups", "ctx")),
        ),
        out_specs=(
            P(("groups", "ctx"), None),
            P("groups", "ctx"),
            P(("groups", "ctx"), None, None),
        ),
        check_vma=False,
    )
```

```python
import functools
import math

import jax
import jax.numpy as jnp
from jax import lax
from jax.experimental import pallas as pl
from jax.experimental.pallas import tpu as pltpu
from jax.sharding import PartitionSpec as P

MESH = pl.DeviceIdType.MESH

H = 16
G = 4
DH = 128
Q_DEV = 96
P_DEV = 16
BLK = 16
CAP = 12


def block_size(total_rows):
    return max((size for size in range(1, 1537) if total_rows % size == 0))


def per_device(queries, new_keys, new_values, prefix_keys, prefix_values, prefix_len, owners):
    per_group = H // G
    device_rank = lax.axis_index("ctx")
    cycle_size = lax.axis_size("ctx")
    all_owners, all_live = (
        lax.all_gather(owners, "ctx", axis=0, tiled=True),
        lax.all_gather(prefix_len, "ctx", axis=0, tiled=True),
    )
    block_count = all_owners.shape[0]
    same_owner = all_owners[:, None] == all_owners[None, :]
    lower = jnp.arange(block_count)[None, :] < jnp.arange(block_count)[:, None]
    ranks = jnp.sum((same_owner & lower).astype(jnp.int32), axis=1)
    match = (all_owners[None, :] == device_rank) & (ranks[None, :] == jnp.arange(CAP)[:, None])
    present = jnp.any(match, axis=1)
    wanted = jnp.sum(jnp.where(match, jnp.arange(block_count)[None, :], 0), axis=1)
    want_token = (wanted[:, None] * BLK + jnp.arange(BLK)[None, :]).reshape(-1)
    row_present = jnp.repeat(present, BLK)
    query_heads = queries.reshape(Q_DEV, G, per_group, DH)
    my_tokens = device_rank * Q_DEV + jnp.arange(Q_DEV)
    scale = DH ** (-0.5)

    def attend_rows(state, piece, global_start, pre_width, fresh_width):
        count_rows = piece.shape[0]
        row_index = global_start + jnp.arange(count_rows)
        width = pre_width + fresh_width
        shard_id = row_index // width
        offset = row_index % width
        is_prefix = offset < pre_width
        live_here = jnp.take(all_live, jnp.clip(shard_id, 0, cycle_size - 1))
        token_pos = shard_id * Q_DEV + offset - pre_width
        visible = jnp.where(
            is_prefix[None, :],
            (offset < live_here)[None, :],
            token_pos[None, :] <= my_tokens[:, None],
        )
        running, totals, accum = state
        keys_part = piece[:, : G * DH].reshape(count_rows, G, DH)
        values_part = piece[:, G * DH :].reshape(count_rows, G, DH)
        scores = (
            jnp.einsum("qgjd,kgd->gjqk", query_heads, keys_part, preferred_element_type=jnp.float32)
            * scale
        )
        scores = jnp.where(visible[None, None], scores, -1e30)
        new_top = jnp.maximum(running, jnp.max(scores, axis=-1))
        weights = jnp.where(visible[None, None], jnp.exp(scores - new_top[..., None]), 0.0)
        factor = jnp.exp(running - new_top)
        totals = totals * factor + jnp.sum(weights, axis=-1)
        accum = accum * factor[..., None] + jnp.einsum(
            "gjqk,kgd->gjqd",
            weights.astype(jnp.bfloat16),
            values_part,
            preferred_element_type=jnp.float32,
        )
        return (new_top, totals, accum)

    def fold_piece(state, piece, start, pre_width, fresh_width):
        count_rows = piece.shape[0]
        step_rows = block_size(count_rows)
        steps_count = count_rows // step_rows
        if steps_count == 1:
            return attend_rows(state, piece, start, pre_width, fresh_width)
        pieces = piece.reshape(steps_count, step_rows, piece.shape[1])

        def advance(carried, inputs):
            block_rows, block_id = inputs
            return (
                attend_rows(
                    carried, block_rows, start + block_id * step_rows, pre_width, fresh_width
                ),
                None,
            )

        state, unused = lax.scan(advance, state, (pieces, jnp.arange(steps_count)))
        return state

    start_state = (
        jnp.full((G, per_group, Q_DEV), -1e30, jnp.float32),
        jnp.zeros((G, per_group, Q_DEV), jnp.float32),
        jnp.zeros((G, per_group, Q_DEV, DH), jnp.float32),
    )
    owned_start = jnp.zeros((CAP * BLK, 2 * G * DH), jnp.bfloat16)
    prefix_rows = jnp.concatenate([prefix_keys, prefix_values], 1)
    fresh_rows = jnp.concatenate([new_keys, new_values], 1)
    stacked = jnp.concatenate([prefix_rows, fresh_rows], 0)
    carried = (start_state, owned_start)
    piece = lax.all_gather(stacked, "ctx", axis=0, tiled=True)
    state = fold_piece(carried[0], piece, jnp.int32(0), P_DEV, Q_DEV)
    count_rows = piece.shape[0]
    width = P_DEV + Q_DEV
    target = want_token // Q_DEV * width + P_DEV + want_token % Q_DEV
    inside = (target >= 0) & (target < count_rows) & row_present
    taken = jnp.take(piece, jnp.clip(target, 0, count_rows - 1), axis=0)
    owned = jnp.where(inside[:, None], taken, carried[1])
    running, totals, accum = state
    attended = (
        (accum / totals[..., None])
        .transpose(2, 0, 1, 3)
        .reshape(Q_DEV, H * DH)
        .astype(jnp.bfloat16)
    )
    log_mass = (running + jnp.log(totals)).reshape(H, Q_DEV)
    owned_cache = owned.reshape(CAP, BLK, 2 * G * DH)
    return (attended, log_mass, owned_cache)


PRE, KEY, VAL = range(3)
NEG = -1e30
VMEM_BYTES = 40 * 1024 * 1024


def fused_kernel(
    A, B, q_hbm, k_ref, v_ref, pk_ref, pv_ref, len_hbm, own_hbm, out_ref, log_ref, cache_ref,
    q_buf, p_buf, k_buf, v_buf, len_ref, own_ref, qt, diff, top, total, accum, row_of, load, send, recv,
):
    n = A * B * 2
    tokens, width = k_ref.shape
    prefix = pk_ref.shape[0]
    per_group = H // G
    lanes = per_group * tokens
    rows = 2 * tokens
    scale = DH ** (-0.5) * math.log2(math.e)
    group, me = lax.axis_index("groups"), lax.axis_index("ctx")
    c = me % 2
    b = (me // 2) % B
    a = me // (2 * B)
    up, down = me + 2 * B, me - 2 * B
    side, twin = me + 2 * (1 - 2 * b), me + 1 - 2 * c
    bufs = (p_buf, k_buf, v_buf)

    def shard(a_, b_, c_):
        return (a_ * B + b_) * 2 + c_

    def move(piece, slot, dest, sem):
        return pltpu.make_async_remote_copy(
            src_ref=bufs[piece].at[slot], dst_ref=bufs[piece].at[slot], send_sem=send.at[sem, slot, piece],
            recv_sem=recv.at[slot, piece], device_id=(group, dest), device_id_type=MESH,
        )

    def arrived(piece, slot):
        move(piece, slot, twin, 0).wait_recv()

    loads = [
        pltpu.make_async_copy(src, dst, load.at[i])
        for i, (src, dst) in enumerate((
            (own_hbm, own_ref), (len_hbm, len_ref),
            (k_ref, k_buf.at[me]), (v_ref, v_buf.at[me]),
            (pk_ref, p_buf.at[me, :, 0:width]), (pv_ref, p_buf.at[me, :, width : 2 * width]), (q_hbm, q_buf),
        ))
    ]
    for copy in loads:
        copy.start()

    barrier = pltpu.get_barrier_semaphore()
    for dest in (side, twin):
        pl.semaphore_signal(barrier, inc=1, device_id=(group, dest), device_id_type=MESH)

    @pl.when(a < A - 1)
    def _():
        pl.semaphore_signal(barrier, inc=1, device_id=(group, up), device_id_type=MESH)

    @pl.when(a > 0)
    def _():
        pl.semaphore_signal(barrier, inc=1, device_id=(group, down), device_id_type=MESH)

    slot_id = lax.broadcasted_iota(jnp.int32, (prefix, DH), 0)
    lane = lax.broadcasted_iota(jnp.int32, (prefix, DH), 1)
    loads[0].wait()
    loads[1].wait()
    owner_row = jnp.full((prefix, DH), -1, jnp.int32)
    for j in range(own_ref.shape[0]):
        owner_row = jnp.where(lane // BLK == j, own_ref[j], owner_row)
    meta = jnp.where(lane < tokens, owner_row, jnp.where(slot_id < len_ref[0], 1, 0))
    p_buf[me, :, 2 * width :] = meta.astype(jnp.float32).astype(jnp.bfloat16)
    cache_ref[...] = jnp.zeros(cache_ref.shape, cache_ref.dtype)

    pl.semaphore_wait(barrier, 2 + jnp.where(a < A - 1, 1, 0) + jnp.where(a > 0, 1, 0))

    def from_below(piece, slot):
        @pl.when(a < A - 1)
        def _():
            move(piece, slot, up, 0).start()

        move(piece, slot, side, 2).start()
        move(piece, slot, twin, 3).start()

    def from_above(piece, slot):
        @pl.when(a > 0)
        def _():
            move(piece, slot, down, 1).start()

        move(piece, slot, side, 2).start()
        move(piece, slot, twin, 3).start()

    for piece, needs in ((PRE, loads[4:6]), (KEY, loads[2:3]), (VAL, loads[3:4])):
        for copy in needs:
            copy.wait()
        from_below(piece, me)

        @pl.when(a > 0)
        def _():
            move(piece, me, down, 1).start()

    loads[6].wait()
    for g in range(G):
        heads = [q_buf[:, (g * per_group + j) * DH : (g * per_group + j + 1) * DH] for j in range(per_group)]
        qt[g] = jnp.concatenate(heads, 0).T
    diff[...] = lax.broadcasted_iota(jnp.int32, (rows, lanes), 0) - lax.broadcasted_iota(jnp.int32, (rows, lanes), 1) % tokens
    top[...] = jnp.full(top.shape, NEG, jnp.float32)
    total[...] = jnp.zeros(total.shape, jnp.float32)
    accum[...] = jnp.zeros(accum.shape, jnp.float32)

    def fold(g, keys, values, visible):
        s = jnp.dot(keys, qt[g], preferred_element_type=jnp.float32) * scale
        if visible is not None:
            s = jnp.where(visible, s, NEG)
        old = top[g : g + 1]
        new = jnp.maximum(old, jnp.max(s, axis=0, keepdims=True))
        w = jnp.exp2(s - new)
        factor = jnp.exp2(old - new)
        top[g : g + 1] = new
        total[g : g + 1] = total[g : g + 1] * factor + jnp.sum(w, axis=0, keepdims=True)
        mixed = lax.dot_general(
            values, w.astype(jnp.bfloat16), (((0,), (0,)), ((), ())), preferred_element_type=jnp.float32
        )
        accum[g] = accum[g] * factor + mixed

    def attend(unit, own=False):
        limit = (me - 2 * unit) * tokens
        for g in range(G):
            at = slice(g * DH, (g + 1) * DH)
            keys = k_buf[pl.ds(2 * unit, 2), :, at].reshape(rows, DH)
            values = v_buf[pl.ds(2 * unit, 2), :, at].reshape(rows, DH)
            fold(g, keys, values, diff[...] <= limit if own else None)

    def relay(piece, slot):
        arrived(piece, slot)
        move(piece, slot, twin, 3).start()

    def direct(piece, d):
        @pl.when(a >= d)
        def _():
            arrived(piece, shard(a - d, b, c))
            from_below(piece, shard(a - d, b, c))

        @pl.when(a + d < A)
        def _():
            arrived(piece, shard(a + d, b, c))
            from_above(piece, shard(a + d, b, c))

    def across(piece, e):
        @pl.when(a >= e)
        def _():
            relay(piece, shard(a - e, 1 - b, c))

        @pl.when((a + e < A) & (e > 0))
        def _():
            relay(piece, shard(a + e, 1 - b, c))

    def stage(e, carry):
        @pl.when((a >= e) & (e > 0))
        def _():
            for piece in (KEY, VAL):
                arrived(piece, shard(a - e, b, 1 - c))
            attend((a - e) * B + b)

        @pl.when(e == A - 1)
        def _():
            def near(a_, carry_):
                @pl.when((a_ - a < A - 1) & (a - a_ < A - 1))
                def _():
                    place_slab(a_)

                return carry_

            lax.fori_loop(0, A, near, 0)

        for piece in (PRE, KEY, VAL):
            direct(piece, e + 1)
        across(PRE, e + 1)
        across(KEY, e)
        across(VAL, e)

        @pl.when(a >= e)
        def _():
            for piece in (KEY, VAL):
                arrived(piece, shard(a - e, 1 - b, 1 - c))

        @pl.when((a >= e) & ((e > 0) | (b > 0)))
        def _():
            attend((a - e) * B + 1 - b)

        @pl.when(e == A - 2)
        def _():
            attend_prefix()

        return carry

    def place_slab(a_):
        @pl.when(a_ > a)
        def _():
            for b_ in range(B):
                for piece in (KEY, VAL):
                    arrived(piece, shard(a_, b_, 1 - c))

        slots, slab = cache_ref.shape[0] * BLK, 2 * B * tokens
        hot = lax.broadcasted_iota(jnp.int32, (slots, slab), 0).astype(jnp.float32) == row_of[a_, 0:1]
        hot = jnp.where(hot, 1.0, 0.0).astype(jnp.bfloat16)
        for at, buf in ((0, k_buf), (width, v_buf)):
            rows_ = buf[pl.ds(a_ * 2 * B, 2 * B)].reshape(slab, width)
            picked = jnp.dot(hot, rows_, preferred_element_type=jnp.float32).astype(jnp.bfloat16)
            cache_ref[:, :, at : at + width] += picked.reshape(slots // BLK, BLK, width)

    def attend_prefix():
        for a_ in range(A):
            for b_ in range(B):
                arrived(PRE, shard(a_, b_, 1 - c))
        count = n * prefix
        whole = lambda lo, hi: p_buf[:, :, lo:hi].reshape(count, hi - lo)
        meta = whole(2 * width, 2 * width + DH).astype(jnp.float32)
        alive = jnp.broadcast_to(meta[:, tokens : tokens + 1], (count, lanes)) > 0.5
        for g in range(G):
            lo = g * DH
            fold(g, whole(lo, lo + DH), whole(width + lo, width + lo + DH), alive)
        lane_ = lax.broadcasted_iota(jnp.int32, (count, DH), 1)
        mine = (meta == me.astype(jnp.float32)) & (lane_ < tokens)
        flag = jnp.where(mine, 1.0, 0.0).astype(jnp.bfloat16)
        share = 1.0 / BLK
        from_, to = (lax.broadcasted_iota(jnp.int32, (DH, DH), i) // BLK for i in range(2))
        before = jnp.where(from_ < to, share, 0.0).astype(jnp.bfloat16)
        at, other = (lax.broadcasted_iota(jnp.int32, (count, count), i) // prefix for i in range(2))
        earlier = jnp.where(other < at, 1.0 / prefix, 0.0).astype(jnp.bfloat16)
        inside = jnp.dot(flag, before, preferred_element_type=jnp.float32)
        past = jnp.dot(earlier, flag, preferred_element_type=jnp.float32).astype(jnp.bfloat16)
        past = jnp.dot(past, jnp.full((DH, DH), share, jnp.bfloat16), preferred_element_type=jnp.float32)
        place = (inside + past) * BLK + (lane_ % BLK).astype(jnp.float32)
        place = jnp.where(mine, place, -1.0)
        for a_ in range(A):
            slab = [place[j * prefix : j * prefix + 8, :tokens] for j in range(2 * B * a_, 2 * B * (a_ + 1))]
            row_of[a_] = jnp.concatenate(slab, 1)

    for piece in (KEY, VAL):
        arrived(piece, twin)
    attend(a * B + b, own=True)
    across(PRE, 0)
    lax.fori_loop(0, A, stage, 0)

    for g in range(G):
        result = (accum[g] / total[g : g + 1]).T
        mass = top[g : g + 1] * math.log(2) + jnp.log(total[g : g + 1])
        for j in range(per_group):
            h = g * per_group + j
            out_ref[:, h * DH : (h + 1) * DH] = result[j * tokens : (j + 1) * tokens].astype(jnp.bfloat16)
            log_ref[h : h + 1] = mass[:, j * tokens : (j + 1) * tokens]

    @pl.when((a == 0) | (a == A - 1))
    def _():
        place_slab(A - 1 - a)

    for piece in (PRE, KEY, VAL):
        for a_ in range(A):
            slot = shard(a_, b, c)

            @pl.when((a_ <= a) & (a < A - 1))
            def _():
                move(piece, slot, up, 0).wait_send()

            @pl.when((a_ >= a) & (a > 0))
            def _():
                move(piece, slot, down, 1).wait_send()

            move(piece, slot, side, 2).wait_send()
            move(piece, slot, twin, 3).wait_send()
            move(piece, shard(a_, 1 - b, c), twin, 3).wait_send()


def write_results(*refs):
    copies = [pltpu.make_async_copy(refs[i], refs[3 + i], refs[6].at[i]) for i in range(3)]
    for copy in copies:
        copy.start()
    for copy in copies:
        copy.wait()


def fused(A, B, queries, new_keys, new_values, prefix_keys, prefix_values, prefix_len, owners):
    n = A * B * 2
    tokens, width = new_keys.shape
    prefix = prefix_keys.shape[0]
    lanes = H // G * tokens
    bf16, f32 = jnp.bfloat16, jnp.float32
    vmem, hbm = pl.BlockSpec(memory_space=pltpu.VMEM), pl.BlockSpec(memory_space=pltpu.HBM)
    assert tokens < DH
    arrays = (queries, new_keys, new_values, prefix_keys, prefix_values)
    results = pl.pallas_call(
        functools.partial(fused_kernel, A, B),
        out_shape=(
            jax.ShapeDtypeStruct((tokens, H * DH), bf16),
            jax.ShapeDtypeStruct((H, tokens), f32),
            jax.ShapeDtypeStruct((CAP, BLK, 2 * width), bf16),
        ),
        in_specs=[hbm] * 7,
        out_specs=(vmem,) * 3,
        scratch_shapes=[
            pltpu.VMEM((tokens, H * DH), bf16),
            pltpu.VMEM((n, prefix, 2 * width + DH), bf16),
            pltpu.VMEM((n, tokens, width), bf16),
            pltpu.VMEM((n, tokens, width), bf16),
            pltpu.SMEM(prefix_len.shape, jnp.int32),
            pltpu.SMEM(owners.shape, jnp.int32),
            pltpu.VMEM((G, DH, lanes), bf16),
            pltpu.VMEM((2 * tokens, lanes), jnp.int32),
            pltpu.VMEM((8, lanes), f32),
            pltpu.VMEM((8, lanes), f32),
            pltpu.VMEM((G, DH, lanes), f32),
            pltpu.VMEM((A, 8, 2 * B * tokens), f32),
            pltpu.SemaphoreType.DMA((7,)),
            pltpu.SemaphoreType.DMA((4, n, 3)),
            pltpu.SemaphoreType.DMA((n, 3)),
        ],
        compiler_params=pltpu.CompilerParams(
            collective_id=0, has_side_effects=True, vmem_limit_bytes=VMEM_BYTES
        ),
    )(*(pltpu.with_memory_space_constraint(x, pltpu.HBM) for x in arrays), prefix_len, pltpu.with_memory_space_constraint(owners, pltpu.HBM))
    return pl.pallas_call(
        write_results,
        out_shape=tuple(jax.ShapeDtypeStruct(x.shape, x.dtype) for x in results),
        in_specs=[vmem] * 3,
        out_specs=(hbm,) * 3,
        scratch_shapes=[pltpu.SemaphoreType.DMA((3,))],
        compiler_params=pltpu.CompilerParams(vmem_limit_bytes=4 * 1024 * 1024),
    )(*results)


def solution(mesh):
    A = 4
    B = mesh.shape["ctx"] // (2 * A)
    body = functools.partial(fused, A, B) if B == 2 else per_device
    return jax.shard_map(
        body,
        mesh=mesh,
        in_specs=(
            P(("groups", "ctx"), None),
            P(("groups", "ctx"), None),
            P(("groups", "ctx"), None),
            P(("groups", "ctx"), None),
            P(("groups", "ctx"), None),
            P(("groups", "ctx")),
            P(("groups", "ctx")),
        ),
        out_specs=(
            P(("groups", "ctx"), None),
            P("groups", "ctx"),
            P(("groups", "ctx"), None, None),
        ),
        check_vma=False,
    )
```

```python
import functools
import math

import jax
import jax.numpy as jnp
from jax import lax
from jax.experimental import pallas as pl
from jax.experimental.pallas import tpu as pltpu
from jax.sharding import PartitionSpec as P

MESH = pl.DeviceIdType.MESH

H = 16
G = 4
DH = 128
Q_DEV = 96
P_DEV = 16
BLK = 16
CAP = 12


def block_size(total_rows):
    return max((size for size in range(1, 1537) if total_rows % size == 0))


def per_device(queries, new_keys, new_values, prefix_keys, prefix_values, prefix_len, owners):
    per_group = H // G
    device_rank = lax.axis_index("ctx")
    cycle_size = lax.axis_size("ctx")
    all_owners, all_live = (
        lax.all_gather(owners, "ctx", axis=0, tiled=True),
        lax.all_gather(prefix_len, "ctx", axis=0, tiled=True),
    )
    block_count = all_owners.shape[0]
    same_owner = all_owners[:, None] == all_owners[None, :]
    lower = jnp.arange(block_count)[None, :] < jnp.arange(block_count)[:, None]
    ranks = jnp.sum((same_owner & lower).astype(jnp.int32), axis=1)
    match = (all_owners[None, :] == device_rank) & (ranks[None, :] == jnp.arange(CAP)[:, None])
    present = jnp.any(match, axis=1)
    wanted = jnp.sum(jnp.where(match, jnp.arange(block_count)[None, :], 0), axis=1)
    want_token = (wanted[:, None] * BLK + jnp.arange(BLK)[None, :]).reshape(-1)
    row_present = jnp.repeat(present, BLK)
    query_heads = queries.reshape(Q_DEV, G, per_group, DH)
    my_tokens = device_rank * Q_DEV + jnp.arange(Q_DEV)
    scale = DH ** (-0.5)

    def attend_rows(state, piece, global_start, pre_width, fresh_width):
        count_rows = piece.shape[0]
        row_index = global_start + jnp.arange(count_rows)
        width = pre_width + fresh_width
        shard_id = row_index // width
        offset = row_index % width
        is_prefix = offset < pre_width
        live_here = jnp.take(all_live, jnp.clip(shard_id, 0, cycle_size - 1))
        token_pos = shard_id * Q_DEV + offset - pre_width
        visible = jnp.where(
            is_prefix[None, :],
            (offset < live_here)[None, :],
            token_pos[None, :] <= my_tokens[:, None],
        )
        running, totals, accum = state
        keys_part = piece[:, : G * DH].reshape(count_rows, G, DH)
        values_part = piece[:, G * DH :].reshape(count_rows, G, DH)
        scores = (
            jnp.einsum("qgjd,kgd->gjqk", query_heads, keys_part, preferred_element_type=jnp.float32)
            * scale
        )
        scores = jnp.where(visible[None, None], scores, -1e30)
        new_top = jnp.maximum(running, jnp.max(scores, axis=-1))
        weights = jnp.where(visible[None, None], jnp.exp(scores - new_top[..., None]), 0.0)
        factor = jnp.exp(running - new_top)
        totals = totals * factor + jnp.sum(weights, axis=-1)
        accum = accum * factor[..., None] + jnp.einsum(
            "gjqk,kgd->gjqd",
            weights.astype(jnp.bfloat16),
            values_part,
            preferred_element_type=jnp.float32,
        )
        return (new_top, totals, accum)

    def fold_piece(state, piece, start, pre_width, fresh_width):
        count_rows = piece.shape[0]
        step_rows = block_size(count_rows)
        steps_count = count_rows // step_rows
        if steps_count == 1:
            return attend_rows(state, piece, start, pre_width, fresh_width)
        pieces = piece.reshape(steps_count, step_rows, piece.shape[1])

        def advance(carried, inputs):
            block_rows, block_id = inputs
            return (
                attend_rows(
                    carried, block_rows, start + block_id * step_rows, pre_width, fresh_width
                ),
                None,
            )

        state, unused = lax.scan(advance, state, (pieces, jnp.arange(steps_count)))
        return state

    start_state = (
        jnp.full((G, per_group, Q_DEV), -1e30, jnp.float32),
        jnp.zeros((G, per_group, Q_DEV), jnp.float32),
        jnp.zeros((G, per_group, Q_DEV, DH), jnp.float32),
    )
    owned_start = jnp.zeros((CAP * BLK, 2 * G * DH), jnp.bfloat16)
    prefix_rows = jnp.concatenate([prefix_keys, prefix_values], 1)
    fresh_rows = jnp.concatenate([new_keys, new_values], 1)
    stacked = jnp.concatenate([prefix_rows, fresh_rows], 0)
    carried = (start_state, owned_start)
    piece = lax.all_gather(stacked, "ctx", axis=0, tiled=True)
    state = fold_piece(carried[0], piece, jnp.int32(0), P_DEV, Q_DEV)
    count_rows = piece.shape[0]
    width = P_DEV + Q_DEV
    target = want_token // Q_DEV * width + P_DEV + want_token % Q_DEV
    inside = (target >= 0) & (target < count_rows) & row_present
    taken = jnp.take(piece, jnp.clip(target, 0, count_rows - 1), axis=0)
    owned = jnp.where(inside[:, None], taken, carried[1])
    running, totals, accum = state
    attended = (
        (accum / totals[..., None])
        .transpose(2, 0, 1, 3)
        .reshape(Q_DEV, H * DH)
        .astype(jnp.bfloat16)
    )
    log_mass = (running + jnp.log(totals)).reshape(H, Q_DEV)
    owned_cache = owned.reshape(CAP, BLK, 2 * G * DH)
    return (attended, log_mass, owned_cache)


PRE, KEY, VAL = range(3)
NEG = -1e30
VMEM_BYTES = 40 * 1024 * 1024


def fused_kernel(
    A, B, q_hbm, k_ref, v_ref, pk_ref, pv_ref, len_hbm, own_hbm, out_ref, log_ref, cache_ref,
    q_buf, p_buf, k_buf, v_buf, len_ref, own_ref, qt, diff, top, total, accum, row_of, load, send, recv,
):
    n = A * B * 2
    tokens, width = k_ref.shape
    prefix = pk_ref.shape[0]
    per_group = H // G
    lanes = per_group * tokens
    rows = 2 * tokens
    scale = DH ** (-0.5) * math.log2(math.e)
    group, me = lax.axis_index("groups"), lax.axis_index("ctx")
    c = me % 2
    b = (me // 2) % B
    a = me // (2 * B)
    up, down = me + 2 * B, me - 2 * B
    side, twin = me + 2 * (1 - 2 * b), me + 1 - 2 * c
    bufs = (p_buf, k_buf, v_buf)

    def shard(a_, b_, c_):
        return (a_ * B + b_) * 2 + c_

    def move(piece, slot, dest, sem):
        return pltpu.make_async_remote_copy(
            src_ref=bufs[piece].at[slot], dst_ref=bufs[piece].at[slot], send_sem=send.at[sem, slot, piece],
            recv_sem=recv.at[slot, piece], device_id=(group, dest), device_id_type=MESH,
        )

    def arrived(piece, slot):
        move(piece, slot, twin, 0).wait_recv()

    loads = [
        pltpu.make_async_copy(src, dst, load.at[i])
        for i, (src, dst) in enumerate((
            (own_hbm, own_ref), (len_hbm, len_ref),
            (k_ref, k_buf.at[me]), (v_ref, v_buf.at[me]),
            (pk_ref, p_buf.at[me, :, 0:width]), (pv_ref, p_buf.at[me, :, width : 2 * width]), (q_hbm, q_buf),
        ))
    ]
    for copy in loads:
        copy.start()

    barrier = pltpu.get_barrier_semaphore()
    for dest in (side, twin):
        pl.semaphore_signal(barrier, inc=1, device_id=(group, dest), device_id_type=MESH)

    @pl.when(a < A - 1)
    def _():
        pl.semaphore_signal(barrier, inc=1, device_id=(group, up), device_id_type=MESH)

    @pl.when(a > 0)
    def _():
        pl.semaphore_signal(barrier, inc=1, device_id=(group, down), device_id_type=MESH)

    slot_id = lax.broadcasted_iota(jnp.int32, (prefix, DH), 0)
    lane = lax.broadcasted_iota(jnp.int32, (prefix, DH), 1)
    loads[0].wait()
    loads[1].wait()
    owner_row = jnp.full((prefix, DH), -1, jnp.int32)
    for j in range(own_ref.shape[0]):
        owner_row = jnp.where(lane // BLK == j, own_ref[j], owner_row)
    meta = jnp.where(lane < tokens, owner_row, jnp.where(slot_id < len_ref[0], 1, 0))
    p_buf[me, :, 2 * width :] = meta.astype(jnp.float32).astype(jnp.bfloat16)
    cache_ref[...] = jnp.zeros(cache_ref.shape, cache_ref.dtype)

    pl.semaphore_wait(barrier, 2 + jnp.where(a < A - 1, 1, 0) + jnp.where(a > 0, 1, 0))

    def to_side(piece, slot, d):
        if piece == KEY:
            @pl.when(d < A - 1)
            def _():
                move(piece, slot, side, 2).start()
        else:
            move(piece, slot, side, 2).start()

    def from_below(piece, slot, d=0):
        @pl.when(a < A - 1)
        def _():
            move(piece, slot, up, 0).start()

        to_side(piece, slot, d)
        move(piece, slot, twin, 3).start()

    def from_above(piece, slot, d=0):
        @pl.when(a > 0)
        def _():
            move(piece, slot, down, 1).start()

        to_side(piece, slot, d)
        move(piece, slot, twin, 3).start()

    for piece, needs in ((PRE, loads[4:6]), (KEY, loads[2:3]), (VAL, loads[3:4])):
        for copy in needs:
            copy.wait()
        from_below(piece, me)

        @pl.when(a > 0)
        def _():
            move(piece, me, down, 1).start()

    loads[6].wait()
    for g in range(G):
        heads = [q_buf[:, (g * per_group + j) * DH : (g * per_group + j + 1) * DH] for j in range(per_group)]
        qt[g] = jnp.concatenate(heads, 0).T
    diff[...] = lax.broadcasted_iota(jnp.int32, (rows, lanes), 0) - lax.broadcasted_iota(jnp.int32, (rows, lanes), 1) % tokens
    top[...] = jnp.full(top.shape, NEG, jnp.float32)
    total[...] = jnp.zeros(total.shape, jnp.float32)
    accum[...] = jnp.zeros(accum.shape, jnp.float32)

    def fold(g, keys, values, visible):
        s = jnp.dot(keys, qt[g], preferred_element_type=jnp.float32) * scale
        if visible is not None:
            s = jnp.where(visible, s, NEG)
        old = top[g : g + 1]
        new = jnp.maximum(old, jnp.max(s, axis=0, keepdims=True))
        w = jnp.exp2(s - new)
        factor = jnp.exp2(old - new)
        top[g : g + 1] = new
        total[g : g + 1] = total[g : g + 1] * factor + jnp.sum(w, axis=0, keepdims=True)
        mixed = lax.dot_general(
            values, w.astype(jnp.bfloat16), (((0,), (0,)), ((), ())), preferred_element_type=jnp.float32
        )
        accum[g] = accum[g] * factor + mixed

    def attend(unit, own=False):
        limit = (me - 2 * unit) * tokens
        for g in range(G):
            at = slice(g * DH, (g + 1) * DH)
            keys = k_buf[pl.ds(2 * unit, 2), :, at].reshape(rows, DH)
            values = v_buf[pl.ds(2 * unit, 2), :, at].reshape(rows, DH)
            fold(g, keys, values, diff[...] <= limit if own else None)

    def relay(piece, slot):
        arrived(piece, slot)
        move(piece, slot, twin, 3).start()

    def direct(piece, d):
        @pl.when(a >= d)
        def _():
            arrived(piece, shard(a - d, b, c))
            from_below(piece, shard(a - d, b, c), d)

        @pl.when(a + d < A)
        def _():
            arrived(piece, shard(a + d, b, c))
            from_above(piece, shard(a + d, b, c), d)

    def across(piece, e):
        @pl.when(a >= e)
        def _():
            relay(piece, shard(a - e, 1 - b, c))

            if piece == KEY:
                @pl.when((e == A - 2) & (a == A - 2))
                def _():
                    move(piece, shard(a - e, 1 - b, c), up, 0).start()

        @pl.when((a + e < A) & (e > 0))
        def _():
            relay(piece, shard(a + e, 1 - b, c))

            if piece == KEY:
                @pl.when((e == A - 2) & (a == 1))
                def _():
                    move(piece, shard(a + e, 1 - b, c), down, 1).start()

    def stage(e, carry):
        @pl.when((a >= e) & (e > 0))
        def _():
            for piece in (KEY, VAL):
                arrived(piece, shard(a - e, b, 1 - c))
            attend((a - e) * B + b)

        @pl.when(e == A - 1)
        def _():
            def near(a_, carry_):
                @pl.when((a_ - a < A - 1) & (a - a_ < A - 1))
                def _():
                    place_slab(a_)

                return carry_

            lax.fori_loop(0, A, near, 0)

        for piece in (PRE, KEY, VAL):
            direct(piece, e + 1)
        across(KEY, e)
        across(VAL, e)
        across(PRE, e + 1)

        @pl.when(a >= e)
        def _():
            for piece in (KEY, VAL):
                arrived(piece, shard(a - e, 1 - b, 1 - c))

        @pl.when((a >= e) & ((e > 0) | (b > 0)))
        def _():
            attend((a - e) * B + 1 - b)

        @pl.when(e == A - 2)
        def _():
            attend_prefix()

        return carry

    def place_slab(a_):
        @pl.when(a_ > a)
        def _():
            for b_ in range(B):
                for piece in (KEY, VAL):
                    arrived(piece, shard(a_, b_, 1 - c))

        slots, slab = cache_ref.shape[0] * BLK, 2 * B * tokens
        hot = lax.broadcasted_iota(jnp.int32, (slots, slab), 0).astype(jnp.float32) == row_of[a_, 0:1]
        hot = jnp.where(hot, 1.0, 0.0).astype(jnp.bfloat16)
        for at, buf in ((0, k_buf), (width, v_buf)):
            rows_ = buf[pl.ds(a_ * 2 * B, 2 * B)].reshape(slab, width)
            picked = jnp.dot(hot, rows_, preferred_element_type=jnp.float32).astype(jnp.bfloat16)
            cache_ref[:, :, at : at + width] += picked.reshape(slots // BLK, BLK, width)

    def attend_prefix():
        for a_ in range(A):
            for b_ in range(B):
                arrived(PRE, shard(a_, b_, 1 - c))
        count = n * prefix
        whole = lambda lo, hi: p_buf[:, :, lo:hi].reshape(count, hi - lo)
        meta = whole(2 * width, 2 * width + DH).astype(jnp.float32)
        alive = jnp.broadcast_to(meta[:, tokens : tokens + 1], (count, lanes)) > 0.5
        for g in range(G):
            lo = g * DH
            fold(g, whole(lo, lo + DH), whole(width + lo, width + lo + DH), alive)
        lane_ = lax.broadcasted_iota(jnp.int32, (count, DH), 1)
        mine = (meta == me.astype(jnp.float32)) & (lane_ < tokens)
        flag = jnp.where(mine, 1.0, 0.0).astype(jnp.bfloat16)
        share = 1.0 / BLK
        from_, to = (lax.broadcasted_iota(jnp.int32, (DH, DH), i) // BLK for i in range(2))
        before = jnp.where(from_ < to, share, 0.0).astype(jnp.bfloat16)
        at, other = (lax.broadcasted_iota(jnp.int32, (count, count), i) // prefix for i in range(2))
        earlier = jnp.where(other < at, 1.0 / prefix, 0.0).astype(jnp.bfloat16)
        inside = jnp.dot(flag, before, preferred_element_type=jnp.float32)
        past = jnp.dot(earlier, flag, preferred_element_type=jnp.float32).astype(jnp.bfloat16)
        past = jnp.dot(past, jnp.full((DH, DH), share, jnp.bfloat16), preferred_element_type=jnp.float32)
        place = (inside + past) * BLK + (lane_ % BLK).astype(jnp.float32)
        place = jnp.where(mine, place, -1.0)
        for a_ in range(A):
            slab = [place[j * prefix : j * prefix + 8, :tokens] for j in range(2 * B * a_, 2 * B * (a_ + 1))]
            row_of[a_] = jnp.concatenate(slab, 1)

    for piece in (KEY, VAL):
        arrived(piece, twin)
    attend(a * B + b, own=True)
    across(PRE, 0)
    lax.fori_loop(0, A, stage, 0)

    for g in range(G):
        result = (accum[g] / total[g : g + 1]).T
        mass = top[g : g + 1] * math.log(2) + jnp.log(total[g : g + 1])
        for j in range(per_group):
            h = g * per_group + j
            out_ref[:, h * DH : (h + 1) * DH] = result[j * tokens : (j + 1) * tokens].astype(jnp.bfloat16)
            log_ref[h : h + 1] = mass[:, j * tokens : (j + 1) * tokens]

    @pl.when((a == 0) | (a == A - 1))
    def _():
        place_slab(A - 1 - a)

    for piece in (PRE, KEY, VAL):
        for a_ in range(A):
            slot = shard(a_, b, c)

            @pl.when((a_ <= a) & (a < A - 1))
            def _():
                move(piece, slot, up, 0).wait_send()

            @pl.when((a_ >= a) & (a > 0))
            def _():
                move(piece, slot, down, 1).wait_send()

            @pl.when((piece != KEY) | ((a - a_ < A - 1) & (a_ - a < A - 1)))
            def _():
                move(piece, slot, side, 2).wait_send()

            move(piece, slot, twin, 3).wait_send()
            move(piece, shard(a_, 1 - b, c), twin, 3).wait_send()

    @pl.when(a == A - 2)
    def _():
        move(KEY, shard(0, 1 - b, c), up, 0).wait_send()

    @pl.when(a == 1)
    def _():
        move(KEY, shard(A - 1, 1 - b, c), down, 1).wait_send()


def write_results(*refs):
    copies = [pltpu.make_async_copy(refs[i], refs[3 + i], refs[6].at[i]) for i in range(3)]
    for copy in copies:
        copy.start()
    for copy in copies:
        copy.wait()


def fused(A, B, queries, new_keys, new_values, prefix_keys, prefix_values, prefix_len, owners):
    n = A * B * 2
    tokens, width = new_keys.shape
    prefix = prefix_keys.shape[0]
    lanes = H // G * tokens
    bf16, f32 = jnp.bfloat16, jnp.float32
    vmem, hbm = pl.BlockSpec(memory_space=pltpu.VMEM), pl.BlockSpec(memory_space=pltpu.HBM)
    assert tokens < DH
    arrays = (queries, new_keys, new_values, prefix_keys, prefix_values)
    results = pl.pallas_call(
        functools.partial(fused_kernel, A, B),
        out_shape=(
            jax.ShapeDtypeStruct((tokens, H * DH), bf16),
            jax.ShapeDtypeStruct((H, tokens), f32),
            jax.ShapeDtypeStruct((CAP, BLK, 2 * width), bf16),
        ),
        in_specs=[hbm] * 7,
        out_specs=(vmem,) * 3,
        scratch_shapes=[
            pltpu.VMEM((tokens, H * DH), bf16),
            pltpu.VMEM((n, prefix, 2 * width + DH), bf16),
            pltpu.VMEM((n, tokens, width), bf16),
            pltpu.VMEM((n, tokens, width), bf16),
            pltpu.SMEM(prefix_len.shape, jnp.int32),
            pltpu.SMEM(owners.shape, jnp.int32),
            pltpu.VMEM((G, DH, lanes), bf16),
            pltpu.VMEM((2 * tokens, lanes), jnp.int32),
            pltpu.VMEM((8, lanes), f32),
            pltpu.VMEM((8, lanes), f32),
            pltpu.VMEM((G, DH, lanes), f32),
            pltpu.VMEM((A, 8, 2 * B * tokens), f32),
            pltpu.SemaphoreType.DMA((7,)),
            pltpu.SemaphoreType.DMA((4, n, 3)),
            pltpu.SemaphoreType.DMA((n, 3)),
        ],
        compiler_params=pltpu.CompilerParams(
            collective_id=0, has_side_effects=True, vmem_limit_bytes=VMEM_BYTES
        ),
    )(*(pltpu.with_memory_space_constraint(x, pltpu.HBM) for x in arrays), prefix_len, pltpu.with_memory_space_constraint(owners, pltpu.HBM))
    return pl.pallas_call(
        write_results,
        out_shape=tuple(jax.ShapeDtypeStruct(x.shape, x.dtype) for x in results),
        in_specs=[vmem] * 3,
        out_specs=(hbm,) * 3,
        scratch_shapes=[pltpu.SemaphoreType.DMA((3,))],
        compiler_params=pltpu.CompilerParams(vmem_limit_bytes=4 * 1024 * 1024),
    )(*results)


def solution(mesh):
    A = 4
    B = mesh.shape["ctx"] // (2 * A)
    body = functools.partial(fused, A, B) if B == 2 else per_device
    return jax.shard_map(
        body,
        mesh=mesh,
        in_specs=(
            P(("groups", "ctx"), None),
            P(("groups", "ctx"), None),
            P(("groups", "ctx"), None),
            P(("groups", "ctx"), None),
            P(("groups", "ctx"), None),
            P(("groups", "ctx")),
            P(("groups", "ctx")),
        ),
        out_specs=(
            P(("groups", "ctx"), None),
            P("groups", "ctx"),
            P(("groups", "ctx"), None, None),
        ),
        check_vma=False,
    )
```
